32 devices in a mesh: groups: 2 (over y), lat: 4 (over z), tok: 2 (over x), sub: 2 (over core).
Axes of the slice: x: 2, y: 2, z: 4, core: 2. Of those that a mesh axis runs over, the one named last changes fastest.
Arguments:
- acts: bfloat16 [4, 768, 2, 4096], P('groups', 'lat', 'sub', 'tok'), parts along dimension 0, may hold values from -6 to 6
- err_grad: bfloat16 [4, 768, 2, 4096], P(('groups', 'tok'), 'lat', 'sub'), parts along dimension 0, may hold values from -6 to 6
- codes: bfloat16 [4, 768, 512], P(('groups', 'tok'), None, 'lat'), parts along dimension 0, may hold values from 0.19921875 to 2
- dec_weight: bfloat16 [1024, 2, 4096], P(('groups', 'lat'), 'sub'), parts along dimension 0, may hold values from -0.0625 to 0.0625
- act_ids: int32 [4, 3, 3], P('groups'), parts along dimension 0, may hold values from 0 to 3, as said below
- act_count: int32 [4, 3], P('groups'), parts along dimension 0, may hold values from 1 to 3
Outputs:
- grad_dec: bfloat16 [1024, 2, 4096], P(('groups', 'lat'), 'sub', 'tok'), parts along dimension 0
- grad_enc: bfloat16 [2, 4096, 1024], P('sub', 'tok', ('groups', 'lat')), parts along dimension 2
The draws below stay inside these ranges and needn't reach their ends.
There are 2 independent parts, one for each index of `groups`. The reference program is written for one: setup_inputs(seed, part) draws one part's arguments, and reference() takes and returns one part's arrays. A program takes and returns all parts, laid end to end along the dimension named above; each array names one. Nothing has to cross between parts.
Inputs may be any that keep to these rules, and one draw needn't show every extreme that they name: In every row act_ids[t, b, :] holds distinct latent block ids; only the first act_count[t, b] of them are active.
All inputs are finite; a program needn't handle non-finite values.
Results may differ from the reference program's by a relative error of at most 0.0049.
Values may be sent and summed in bfloat16 or wider, within the bound.
No kernel may reach another device: no remote copies, remote signals or barrier semaphores. Data moves between devices by JAX's collectives and lax.ppermute only.
A program may use at most 64 MiB of HBM per device.

```python
import jax
import jax.numpy as jnp
from jax import lax

D = 8192
BLK = 128
TBLK = 256
TBD = 3
ROWS = 768
TGRP = 2
NHALF = 2
DHALF = 4096
LATENTS = 512
MAXA = 3
N_LAT = 4


def draw_act_ids(key, part):
    key = jax.random.fold_in(key, 11)
    first_key, second_key = jax.random.split(key)
    popular = jax.random.randint(first_key, (N_LAT,), 0, 4) * 300
    noise = jax.random.randint(second_key, (TGRP, TBD, N_LAT), 0, 1024)
    block_index = jnp.arange(N_LAT, dtype=jnp.int32)
    ends = (block_index == 0) | (block_index == N_LAT - 1)
    first_row = (jnp.arange(TGRP)[:, None, None] == 0) & (jnp.arange(TBD)[None, :, None] == 0)
    scores = noise + popular[None, None, :] + jnp.where(first_row & ends[None, None, :], 100000, 0)
    scores = scores * N_LAT + block_index[None, None, :]
    return lax.top_k(scores, MAXA)[1].astype(jnp.int32)


def draw_act_count(key, part):
    key = jax.random.fold_in(key, 12)
    first_key, second_key, third_key = jax.random.split(key, 3)
    total = TGRP * TBD
    counts = jax.random.randint(first_key, (total,), 1, MAXA + 1)
    place = jax.random.randint(second_key, (), 0, total)
    offset = jax.random.randint(third_key, (), 1, total)
    low_place = (place + offset) % total
    position = jnp.arange(total)
    counts = jnp.where(position == place, MAXA, counts)
    counts = jnp.where(position == low_place, 1, counts)
    return counts.reshape(TGRP, TBD).astype(jnp.int32)


def spiked(result, own_key, source, target, blocks, factor):
    owner, partner = [(jnp.arange(result.shape[dim]) // (result.shape[dim] // blocks)).reshape([-1 if axis == dim else 1 for axis in range(result.ndim)]) for dim in (source, target)]
    chosen = jax.random.permutation(own_key, blocks)[partner]
    strong = (owner == chosen) | (owner == (partner + blocks // 2) % blocks)
    return jnp.where(strong, factor * result, result)


def block_levels(key, shape, cuts, least, largest):
    def one(dim, parts):
        draws = jax.random.uniform(jax.random.fold_in(jax.random.fold_in(key, 6), dim), (parts,), jnp.float32, least / len(cuts), largest / len(cuts))
        return jnp.repeat(jnp.exp(draws), shape[dim] // parts).reshape((-1,) + (1,) * (len(shape) - dim - 1))

    factor_of = one(*cuts[0])
    for cut in cuts[1:]:
        factor_of = factor_of * one(*cut)
    return factor_of


def gaussian(key, dims, width, most, cuts=(), held_as=jnp.bfloat16):
    values = jax.random.normal(key, dims, jnp.float32) * width
    if len(cuts) > 0:
        values = block_levels(key, dims, cuts, -0.22, 0.18) * values
    return jnp.clip(values, min=-most, max=most).astype(held_as)


def noise_with(rng, shape, spread, bound, cuts, heavy, held_as=jnp.bfloat16):
    array = spread * jax.random.normal(rng, shape, jnp.float32)
    if cuts:
        array = array * block_levels(rng, shape, cuts, -0.22, 0.18)
    return jnp.clip(spiked(array, jax.random.fold_in(rng, 3), *heavy), -bound, bound).astype(held_as)


def setup_inputs(seed: int = 0, part: int = 0) -> dict:
    seeds = jax.random.split(jax.random.key(seed), 7)
    part_keys = jax.random.split(jax.random.fold_in(seeds[6], part), 7)
    acts = gaussian(part_keys[0], (TGRP, ROWS, NHALF, DHALF), 1.0, 6.0, ((1, 4), (2, 2), (3, 2)))
    err_grad = noise_with(part_keys[1], (TGRP, ROWS, NHALF, DHALF), 1.0, 6.0, ((0, 2), (1, 4), (2, 2)), (0, 3, 2, 2.0))
    codes = jnp.clip(0.19921875 + 1.8007812 * jax.random.uniform(part_keys[2], (TGRP, ROWS, LATENTS), jnp.float32) ** block_levels(part_keys[2], (TGRP, ROWS, LATENTS), ((0, 2), (2, 4)), -0.2, 0.2), 0.19921875, 2.0).astype(jnp.bfloat16)
    dec_weight = gaussian(part_keys[3], (LATENTS, NHALF, DHALF), D ** -0.5, 0.0625, ((0, 4), (1, 2)))
    act_ids = draw_act_ids(jax.random.fold_in(jax.random.fold_in(seeds[6], part), 71), part)
    act_count = draw_act_count(jax.random.fold_in(jax.random.fold_in(seeds[6], part), 71), part)
    return dict(acts=acts, err_grad=err_grad, codes=codes, dec_weight=dec_weight, act_ids=act_ids, act_count=act_count)


def reference(acts, err_grad, codes, dec_weight, act_ids, act_count):
    slot_index = jnp.arange(MAXA, dtype=jnp.int32)
    valid = slot_index[None, None, :] < act_count[:, :, None]
    block_index = jnp.arange(N_LAT, dtype=jnp.int32)
    hit = (act_ids[:, :, :, None] == block_index[None, None, None, :]) & valid[:, :, :, None]
    active = jnp.any(hit, axis=2).astype(jnp.float32)
    row_mask = jnp.repeat(jnp.repeat(active, TBLK, axis=1), BLK, axis=2)
    row_mask = row_mask.reshape(TGRP * ROWS, LATENTS)
    grad_rows = err_grad.reshape(TGRP * ROWS, NHALF * DHALF)
    act_rows = acts.reshape(TGRP * ROWS, NHALF * DHALF)
    weight_rows = dec_weight.reshape(LATENTS, NHALF * DHALF)
    dlat = lax.dot_general(grad_rows, weight_rows, (((1,), (1,)), ((), ())), preferred_element_type=jnp.float32)
    dcodes = (dlat * row_mask).astype(jnp.bfloat16)
    used_codes = jnp.where(row_mask > 0, codes.reshape(TGRP * ROWS, LATENTS), jnp.zeros((), jnp.bfloat16))
    grad_dec = lax.dot_general(used_codes, grad_rows, (((0,), (0,)), ((), ())), preferred_element_type=jnp.float32)
    grad_enc = lax.dot_general(act_rows, dcodes, (((0,), (0,)), ((), ())), preferred_element_type=jnp.float32)
    grad_dec = grad_dec.astype(jnp.bfloat16).reshape(LATENTS, NHALF, DHALF)
    grad_enc = grad_enc.astype(jnp.bfloat16).reshape(NHALF, DHALF, LATENTS)
    return (grad_dec, grad_enc)
```

```python
import jax
import jax.numpy as jnp
from jax import lax
from jax.sharding import PartitionSpec as P

TBLK = 256
CONTRACT_LAST = (((1,), (1,)), ((), ()))
CONTRACT_ROWS = (((0,), (0,)), ((), ()))


def dot32(left, right, dims):
    return lax.dot_general(left, right, dims, preferred_element_type=jnp.float32)


def valid_ids(act_ids, act_count):
    slot = jnp.arange(act_ids.shape[2], dtype=jnp.int32)
    return jnp.where(slot[None, None, :] < act_count[:, :, None], act_ids, -1)


def row_hits(ids, first_row, rows, block):
    on = jnp.any(ids == block, axis=2)
    tile = (first_row + jnp.arange(rows, dtype=jnp.int32)) // TBLK
    hit = on[:, :, None] & (tile[None, None, :] == jnp.arange(ids.shape[1])[None, :, None])
    return jnp.any(hit, axis=1).astype(jnp.float32)


def shards_line(acts, err_grad, codes, dec_weight, act_ids, act_count):
    z = lax.axis_index("lat")
    x = lax.axis_index("tok")
    rows = err_grad.shape[1]
    lat = dec_weight.shape[0]
    width = acts.shape[3]
    swap = [(0, 1), (1, 0)]
    up = [(0, 1), (1, 2), (2, 3)]
    down = [(3, 2), (2, 1), (1, 0)]

    def send(value, axis, pairs):
        return lax.ppermute(value, axis, pairs)

    w_own = lax.dynamic_slice_in_dim(dec_weight.reshape(lat, -1), x * width, width, 1)
    w_far = send(w_own, "lat", [(0, 3), (3, 0)])
    w_two = send(w_own, "lat", [(0, 2), (1, 3), (2, 0), (3, 1)])
    w_prev = send(w_own, "lat", up)
    w_next = send(w_own, "lat", down)

    err = err_grad.reshape(rows, -1)
    err_own = lax.dynamic_slice_in_dim(err, x * width, width, 1)
    err_other = send(lax.dynamic_slice_in_dim(err, (1 - x) * width, width, 1), "tok", swap)

    ids = valid_ids(act_ids, act_count)

    code_hits = row_hits(lax.dynamic_slice_in_dim(ids, x, 1, 0), 0, codes.shape[1], z)
    used = codes[0] * code_hits.astype(jnp.bfloat16).T
    codes_own = lax.all_to_all(used, "lat", split_axis=0, concat_axis=1, tiled=True)
    codes_other = send(codes_own, "tok", swap)
    dec_part = dot32(codes_own, err_own, CONTRACT_ROWS) + dot32(codes_other, err_other, CONTRACT_ROWS)
    grad_dec = lax.psum_scatter(
        dec_part.astype(jnp.bfloat16), "lat", scatter_dimension=0, tiled=True
    )

    act_rows = acts.reshape(2 * rows, width)

    def enc_terms(weights, blocks):
        w = jnp.concatenate(weights, axis=0) if len(weights) > 1 else weights[0]
        part_own = dot32(err_own, w, CONTRACT_LAST)
        part_other = dot32(err_other, w, CONTRACT_LAST)
        first = jnp.where(x == 0, part_own, part_other)
        second = jnp.where(x == 0, part_other, part_own)
        part = jnp.concatenate([first, second], axis=0)
        part = part + send(part, "sub", swap)
        part = part + send(part, "tok", swap)
        hits = [row_hits(ids, z * rows, rows, block).reshape(2 * rows, 1) for block in blocks]
        hits = jnp.concatenate([jnp.broadcast_to(h, (2 * rows, lat)) for h in hits], axis=1)
        dcodes = (part * hits).astype(jnp.bfloat16)
        return [
            dot32(act_rows, dcodes[:, i * lat : (i + 1) * lat], CONTRACT_ROWS)
            for i in range(len(blocks))
        ]

    (far,) = enc_terms([w_far], [jnp.where(z == 0, 3, 0)])
    got_far = send(far.astype(jnp.bfloat16), "lat", [(0, 1), (3, 2)])
    (two,) = enc_terms([w_two], [lax.rem(z + 2, 4)])
    two = (two + got_far.astype(jnp.float32)).astype(jnp.bfloat16)
    two_up = send(two, "lat", [(0, 1), (1, 2)])
    two_down = send(two, "lat", [(3, 2), (2, 1)])
    nxt, prev, own = enc_terms([w_next, w_prev, w_own], [z + 1, z - 1, z])
    nxt = (nxt + two_up.astype(jnp.float32)).astype(jnp.bfloat16)
    prev = (prev + two_down.astype(jnp.float32)).astype(jnp.bfloat16)
    from_prev = send(nxt, "lat", up)
    from_next = send(prev, "lat", down)
    grad_enc = own + from_prev.astype(jnp.float32) + from_next.astype(jnp.float32)
    return grad_dec[:, None, :], grad_enc.astype(jnp.bfloat16)[None]


def shards_any(acts, err_grad, codes, dec_weight, act_ids, act_count):
    z = lax.axis_index("lat")
    x = lax.axis_index("tok")
    rows = err_grad.shape[1]
    lat = dec_weight.shape[0]
    width = acts.shape[3]
    groups = acts.shape[0]
    blocks = lax.axis_size("lat")
    w_own = lax.dynamic_slice_in_dim(dec_weight.reshape(lat, -1), x * width, width, 1)
    w_all = lax.all_gather(w_own, "lat", axis=0, tiled=True)
    err = lax.all_to_all(err_grad, "tok", split_axis=3, concat_axis=0, tiled=True)
    err = err.reshape(groups * rows, width)
    ids = valid_ids(act_ids, act_count)
    code_hits = row_hits(lax.dynamic_slice_in_dim(ids, x, 1, 0), 0, codes.shape[1], z)
    used = codes[0] * code_hits.astype(jnp.bfloat16).T
    used = lax.all_to_all(used, "lat", split_axis=0, concat_axis=1, tiled=True)
    used = lax.all_gather(used, "tok", axis=0, tiled=True)
    dec_part = dot32(used, err, CONTRACT_ROWS)
    grad_dec = lax.psum_scatter(dec_part, "lat", scatter_dimension=0, tiled=True)
    dlat = lax.psum(dot32(err, w_all, CONTRACT_LAST), ("tok", "sub"))
    hits = [row_hits(ids, z * rows, rows, block).reshape(groups * rows, 1) for block in range(blocks)]
    hits = jnp.concatenate([jnp.broadcast_to(h, (groups * rows, lat)) for h in hits], axis=1)
    dcodes = (dlat * hits).astype(jnp.bfloat16)
    enc_part = dot32(acts.reshape(groups * rows, width), dcodes, CONTRACT_ROWS)
    grad_enc = lax.psum_scatter(enc_part, "lat", scatter_dimension=1, tiled=True)
    return grad_dec.astype(jnp.bfloat16)[:, None, :], grad_enc.astype(jnp.bfloat16)[None]


def solution(mesh):
    line = mesh.shape["lat"] == 4 and mesh.shape["tok"] == 2
    return jax.shard_map(
        shards_line if line else shards_any,
        mesh=mesh,
        in_specs=(
            P("groups", "lat", "sub", "tok"),
            P(("groups", "tok"), "lat", "sub", None),
            P(("groups", "tok"), None, "lat"),
            P(("groups", "lat"), "sub", None),
            P("groups", None, None),
            P("groups", None),
        ),
        out_specs=(P(("groups", "lat"), "sub", "tok"), P("sub", "tok", ("groups", "lat"))),
        check_vma=False,
    )
```

```python
import jax
import jax.numpy as jnp
from jax import lax
from jax.sharding import PartitionSpec as P

TBLK = 256
CONTRACT_LAST = (((1,), (1,)), ((), ()))
CONTRACT_ROWS = (((0,), (0,)), ((), ()))


def dot32(left, right, dims):
    return lax.dot_general(left, right, dims, preferred_element_type=jnp.float32)


def valid_ids(act_ids, act_count):
    slot = jnp.arange(act_ids.shape[2], dtype=jnp.int32)
    return jnp.where(slot[None, None, :] < act_count[:, :, None], act_ids, -1)


def row_hits(ids, first_row, rows, block):
    on = jnp.any(ids == block, axis=2)
    tile = (first_row + jnp.arange(rows, dtype=jnp.int32)) // TBLK
    hit = on[:, :, None] & (tile[None, None, :] == jnp.arange(ids.shape[1])[None, :, None])
    return jnp.any(hit, axis=1).astype(jnp.float32)


def after(value, *others):
    return lax.optimization_barrier((value,) + others)[0]


def shards_line(acts, err_grad, codes, dec_weight, act_ids, act_count):
    z = lax.axis_index("lat")
    x = lax.axis_index("tok")
    rows = err_grad.shape[1]
    lat = dec_weight.shape[0]
    width = acts.shape[3]
    swap = [(0, 1), (1, 0)]
    up = [(0, 1), (1, 2), (2, 3)]
    down = [(3, 2), (2, 1), (1, 0)]

    def send(value, axis, pairs):
        return lax.ppermute(value, axis, pairs)

    codes_own = lax.all_to_all(
        codes.reshape(4, rows, lat), "lat", split_axis=0, concat_axis=0, tiled=True
    )
    codes_other = send(codes_own, "tok", swap)

    codes_own, weights = lax.optimization_barrier((codes_own, dec_weight.reshape(lat, -1)))
    w_own = lax.dynamic_slice_in_dim(weights, x * width, width, 1)
    w_prev = send(w_own, "lat", [(i, (i + 1) % 4) for i in range(4)])
    w_next = send(w_own, "lat", [(i, (i + 3) % 4) for i in range(4)])

    err = err_grad.reshape(rows, -1)
    err_own = lax.dynamic_slice_in_dim(err, x * width, width, 1)
    err_other = send(lax.dynamic_slice_in_dim(err, (1 - x) * width, width, 1), "tok", swap)

    ids = valid_ids(act_ids, act_count)
    far_block = jnp.where(z == 0, 3, 0)
    two_block = lax.rem(z + 2, 4)
    hits = [row_hits(ids, z * rows, rows, lax.rem(z + d, 4)) for d in range(4)]

    def masked(value, hit):
        return value * hit.reshape(2 * rows, 1)

    all_hits = jnp.stack([row_hits(ids, z * rows, rows, block) for block in range(4)])
    codes_own = codes_own.astype(jnp.float32) * all_hits[:, x, :, None]
    codes_other = codes_other.astype(jnp.float32) * all_hits[:, 1 - x, :, None]
    dec_terms = lax.dot_general(
        codes_own.astype(jnp.bfloat16), err_own, (((1,), (0,)), ((), ())),
        preferred_element_type=jnp.float32,
    ) + lax.dot_general(
        codes_other.astype(jnp.bfloat16), err_other, (((1,), (0,)), ((), ())),
        preferred_element_type=jnp.float32,
    )

    act_rows = acts.reshape(2 * rows, width)

    def latent_grads(w, hit_list):
        part_own = dot32(err_own, w, CONTRACT_LAST)
        part_other = dot32(err_other, w, CONTRACT_LAST)
        first = jnp.where(x == 0, part_own, part_other)
        second = jnp.where(x == 0, part_other, part_own)
        part = jnp.concatenate([first, second], axis=0)
        part = part + send(part, "sub", swap)
        part = part + send(part, "tok", swap)
        return [
            masked(part[:, i * lat : (i + 1) * lat], hit).astype(jnp.bfloat16)
            for i, hit in enumerate(hit_list)
        ]

    def enc_of(dcodes):
        return dot32(act_rows, dcodes, CONTRACT_ROWS)

    def dec_of(block):
        return lax.dynamic_index_in_dim(dec_terms, block, 0, keepdims=False)

    def add_send(term, got, pairs):
        value = term if got is None else term + got.astype(jnp.float32)
        return send(value.astype(jnp.bfloat16), "lat", pairs)

    far_up_down = [(0, 1), (3, 2)]
    two_up, two_down = [(0, 1), (1, 2)], [(3, 2), (2, 1)]
    fwd_up, fwd_down = [(1, 2), (2, 3)], [(2, 1), (1, 0)]

    dec_far = add_send(dec_of(far_block), None, far_up_down)
    w_next, w_prev = after(w_next, dec_terms), after(w_prev, dec_terms)
    d_own, d_next, d_prev = latent_grads(
        jnp.concatenate([w_own, w_next, w_prev], axis=0), [hits[0], hits[1], hits[3]]
    )
    enc_far = add_send(enc_of(jnp.where(z == 0, d_prev, d_next)), None, far_up_down)
    w_two = jnp.where(z < 2, send(w_next, "lat", fwd_down), send(w_prev, "lat", fwd_up))

    dec_two = (dec_of(two_block) + dec_far.astype(jnp.float32)).astype(jnp.bfloat16)
    dec_up, dec_down = send(dec_two, "lat", two_up), send(dec_two, "lat", two_down)
    (d_two,) = latent_grads(w_two, hits[2:3])
    enc_two = (enc_of(d_two) + enc_far.astype(jnp.float32)).astype(jnp.bfloat16)
    enc_up, enc_down = send(enc_two, "lat", two_up), send(enc_two, "lat", two_down)

    dec_prev = add_send(dec_of(jnp.minimum(z + 1, 3)), dec_up, up)
    dec_next = add_send(dec_of(jnp.maximum(z - 1, 0)), dec_down, down)
    enc_prev = add_send(enc_of(d_next), enc_up, up)
    enc_next = add_send(enc_of(d_prev), enc_down, down)

    grad_dec = dec_of(z) + dec_prev.astype(jnp.float32) + dec_next.astype(jnp.float32)
    grad_enc = enc_of(d_own) + enc_prev.astype(jnp.float32) + enc_next.astype(jnp.float32)
    return grad_dec.astype(jnp.bfloat16)[:, None, :], grad_enc.astype(jnp.bfloat16)[None]


def shards_any(acts, err_grad, codes, dec_weight, act_ids, act_count):
    z = lax.axis_index("lat")
    x = lax.axis_index("tok")
    rows = err_grad.shape[1]
    lat = dec_weight.shape[0]
    width = acts.shape[3]
    groups = acts.shape[0]
    blocks = lax.axis_size("lat")
    w_own = lax.dynamic_slice_in_dim(dec_weight.reshape(lat, -1), x * width, width, 1)
    w_all = lax.all_gather(w_own, "lat", axis=0, tiled=True)
    err = lax.all_to_all(err_grad, "tok", split_axis=3, concat_axis=0, tiled=True)
    err = err.reshape(groups * rows, width)
    ids = valid_ids(act_ids, act_count)
    code_hits = row_hits(lax.dynamic_slice_in_dim(ids, x, 1, 0), 0, codes.shape[1], z)
    used = codes[0] * code_hits.astype(jnp.bfloat16).T
    used = lax.all_to_all(used, "lat", split_axis=0, concat_axis=1, tiled=True)
    used = lax.all_gather(used, "tok", axis=0, tiled=True)
    dec_part = dot32(used, err, CONTRACT_ROWS)
    grad_dec = lax.psum_scatter(dec_part, "lat", scatter_dimension=0, tiled=True)
    dlat = lax.psum(dot32(err, w_all, CONTRACT_LAST), ("tok", "sub"))
    hits = [row_hits(ids, z * rows, rows, block).reshape(groups * rows, 1) for block in range(blocks)]
    hits = jnp.concatenate([jnp.broadcast_to(h, (groups * rows, lat)) for h in hits], axis=1)
    dcodes = (dlat * hits).astype(jnp.bfloat16)
    enc_part = dot32(acts.reshape(groups * rows, width), dcodes, CONTRACT_ROWS)
    grad_enc = lax.psum_scatter(enc_part, "lat", scatter_dimension=1, tiled=True)
    return grad_dec.astype(jnp.bfloat16)[:, None, :], grad_enc.astype(jnp.bfloat16)[None]


def solution(mesh):
    line = mesh.shape["lat"] == 4 and mesh.shape["tok"] == 2
    return jax.shard_map(
        shards_line if line else shards_any,
        mesh=mesh,
        in_specs=(
            P("groups", "lat", "sub", "tok"),
            P(("groups", "tok"), "lat", "sub", None),
            P(("groups", "tok"), None, "lat"),
            P(("groups", "lat"), "sub", None),
            P("groups", None, None),
            P("groups", None),
        ),
        out_specs=(P(("groups", "lat"), "sub", "tok"), P("sub", "tok", ("groups", "lat"))),
        check_vma=False,
    )
```

```python
import functools

import jax
import jax.numpy as jnp
from jax import lax
from jax.experimental import pallas as pl
from jax.experimental.pallas import tpu as pltpu
from jax.sharding import PartitionSpec as P

TBLK = 256
MERGED = False
ORDER = {
    "dec_down": ("enc_two",),
    "dec_far": ("enc_far_in",),
    "dec_up": ("enc_two",),
    "tok_near": ("up", "down",),
    "tok_two": ("dec_two",),
    "w_next": ("dec",),
    "w_next_in": ("codes",),
    "w_prev": ("dec",),
}
CONTRACT_LAST = (((1,), (1,)), ((), ()))
PLAIN = (((1,), (0,)), ((), ()))
CONTRACT_ROWS = (((0,), (0,)), ((), ()))


def dot32(left, right, dims):
    return lax.dot_general(left, right, dims, preferred_element_type=jnp.float32)


def local_call(body, out_shape, scalars, *args):
    vmem = pl.BlockSpec(memory_space=pltpu.VMEM)
    return pl.pallas_call(
        body,
        out_shape=out_shape,
        in_specs=[pl.BlockSpec(memory_space=pltpu.SMEM)] + [vmem] * len(args),
        out_specs=jax.tree.map(lambda _: vmem, out_shape),
        compiler_params=pltpu.CompilerParams(vmem_limit_bytes=32 * 2**20),
        cost_estimate=pl.CostEstimate(flops=0, bytes_accessed=0, transcendentals=0),
    )(jnp.stack(scalars).astype(jnp.int32), *args)


def turned(value):
    return value.astype(jnp.float32).T.astype(jnp.bfloat16)


def dec_body(far_ref, own_ref, other_ref, err_own_ref, err_other_ref, out_ref, first_ref):
    for j in range(out_ref.shape[0]):
        out_ref[j] = dot32(turned(own_ref[j]), err_own_ref[...], PLAIN) + dot32(
            turned(other_ref[j]), err_other_ref[...], PLAIN
        )
    first_ref[...] = out_ref[far_ref[0]].astype(jnp.bfloat16)


def dlat_body(place_ref, own_ref, other_ref, *refs):
    place, out_ref = place_ref[0], refs[-1]
    for i, w_ref in enumerate(refs[:-1]):
        lanes = slice(i * w_ref.shape[0], (i + 1) * w_ref.shape[0])
        out_ref[place, :, lanes] = dot32(own_ref[...], w_ref[...], CONTRACT_LAST)
        out_ref[1 - place, :, lanes] = dot32(other_ref[...], w_ref[...], CONTRACT_LAST)


def enc_body(core_ref, acts_ref, mine_ref, other_ref, out_ref):
    core = core_ref[0]
    total = dot32(turned(mine_ref[...]), acts_ref[core], PLAIN)
    total += dot32(turned(other_ref[...]), acts_ref[1 - core], PLAIN)
    out_ref[...] = total.astype(out_ref.dtype)


def valid_ids(act_ids, act_count):
    slot = jnp.arange(act_ids.shape[2], dtype=jnp.int32)
    return jnp.where(slot[None, None, :] < act_count[:, :, None], act_ids, -1)


def row_hits(ids, first_row, rows, block):
    on = jnp.any(ids == block, axis=2)
    tile = (first_row + jnp.arange(rows, dtype=jnp.int32)) // TBLK
    hit = on[:, :, None] & (tile[None, None, :] == jnp.arange(ids.shape[1])[None, :, None])
    return jnp.any(hit, axis=1).astype(jnp.float32)


def shards_line(acts, err_grad, codes, dec_weight, act_ids, act_count):
    z = lax.axis_index("lat")
    x = lax.axis_index("tok")
    c = lax.axis_index("sub")
    rows = err_grad.shape[1]
    lat = dec_weight.shape[0]
    width = acts.shape[3]
    swap = [(0, 1), (1, 0)]
    ring = [(0, 1), (1, 2), (2, 3), (3, 0)]
    up, down = [(0, 1), (1, 2), (2, 3)], [(3, 2), (2, 1), (1, 0)]
    up_two, down_two = [(0, 1), (1, 2)], [(3, 2), (2, 1)]
    up_on, down_on = [(1, 2), (2, 3)], [(2, 1), (1, 0)]
    inward = [(0, 1), (3, 2)]

    ids = valid_ids(act_ids, act_count)
    far_block = jnp.where(z == 0, 3, 0)
    two_block = lax.rem(z + 2, 4)
    act_rows = acts.reshape(2, rows, width)
    err_rows = err_grad.reshape(rows, -1)
    block = jax.ShapeDtypeStruct((lat, width), jnp.float32)
    block16 = jax.ShapeDtypeStruct((lat, width), jnp.bfloat16)
    steps, done = {}, {}

    def get(name):
        if name not in done:
            value = steps[name]()
            others = [get(other) for other in ORDER.get(name, ())]
            done[name] = lax.optimization_barrier((value, *others))[0] if others else value
        return done[name]

    def step(name, make):
        steps[name] = make

    def send(name, source, axis, pairs):
        step(name + "_in", source)
        step(name, lambda: lax.ppermute(get(name + "_in"), axis, pairs))

    def add32(term, got):
        return (term + got.astype(jnp.float32)).astype(jnp.bfloat16)

    step("weights", lambda: dec_weight.reshape(lat, -1))
    step("w_own", lambda: lax.dynamic_slice_in_dim(get("weights"), x * width, width, 1))
    send("w_prev", lambda: get("w_own"), "lat", ring)
    send("w_next", lambda: get("w_own"), "lat", [(b, a) for a, b in ring])

    step("err_own", lambda: lax.dynamic_slice_in_dim(err_rows, x * width, width, 1))
    send("err", lambda: lax.dynamic_slice_in_dim(err_rows, (1 - x) * width, width, 1), "tok", swap)

    step("codes_in", lambda: codes.reshape(4, rows, lat))
    step("codes", lambda: lax.all_to_all(get("codes_in"), "lat", split_axis=0, concat_axis=0, tiled=True))
    send("codes_other", lambda: get("codes"), "tok", swap)

    def used(value, group):
        all_hits = jnp.stack([row_hits(ids, z * rows, rows, b) for b in range(4)])
        hit = lax.dynamic_index_in_dim(all_hits, group, 1, keepdims=False)
        return value * hit[:, :, None].astype(jnp.bfloat16)

    step("used_own", lambda: used(get("codes"), x))
    step(
        "dec",
        lambda: local_call(
            dec_body,
            (jax.ShapeDtypeStruct((4, lat, width), jnp.float32), block16),
            [far_block], get("used_own"), used(get("codes_other"), 1 - x), get("err_own"), get("err"),
        ),
    )

    def dec_of(b):
        return lax.dynamic_index_in_dim(get("dec")[0], b, 0, keepdims=False)

    if MERGED:
        send("up", lambda: jnp.where(z == 0, get("dec")[1], get("w_prev")), "lat", up)
        send("down", lambda: jnp.where(z == 3, get("dec")[1], get("w_next")), "lat", down)

        def far_term():
            got = jnp.where(z == 1, get("up"), get("down"))
            return jnp.where((z == 1) | (z == 2), got, jnp.zeros((), jnp.bfloat16))

        step("dec_far", far_term)
    else:
        send("up", lambda: get("w_prev"), "lat", up_on)
        send("down", lambda: get("w_next"), "lat", down_on)
        send("dec_far", lambda: get("dec")[1], "lat", inward)
    step("w_two", lambda: jnp.where(z < 2, get("down"), get("up")))

    def latent_grads(tag, names, blocks):
        def part():
            weights = [get(name) for name in names]
            out = jax.ShapeDtypeStruct((2, rows, lat * len(weights)), jnp.float32)
            return local_call(dlat_body, out, [c ^ x], get("err_own"), get("err"), *weights)

        def mine():
            total, cols = get("sums" + tag) + get("tok" + tag), []
            for i, b in enumerate(blocks):
                hit = lax.dynamic_index_in_dim(row_hits(ids, z * rows, rows, b), c, 0, keepdims=False)
                cols.append((total[:, i * lat : (i + 1) * lat] * hit[:, None]).astype(jnp.bfloat16))
            return jnp.concatenate(cols, axis=1)

        step("part" + tag, part)
        send("sub" + tag, lambda: get("part" + tag)[1], "sub", swap)
        step("sums" + tag, lambda: get("part" + tag)[0] + get("sub" + tag))
        send("tok" + tag, lambda: get("sums" + tag), "tok", swap)
        step("mine" + tag, mine)
        send("other" + tag, lambda: get("mine" + tag), "sub", swap)

    latent_grads("_near", ["w_own", "w_next", "w_prev"], [z, lax.rem(z + 1, 4), lax.rem(z + 3, 4)])
    latent_grads("_two", ["w_two"], [two_block])

    def enc_of(tag, pick, out=block):
        return local_call(enc_body, out, [c], act_rows, pick(get("mine" + tag)), pick(get("other" + tag)))

    def near(i):
        return lambda part: part[:, i * lat : (i + 1) * lat]

    send(
        "enc_far",
        lambda: enc_of("_near", lambda part: jnp.where(z == 0, near(2)(part), near(1)(part)), block16),
        "lat", inward,
    )
    step("dec_two", lambda: add32(dec_of(two_block), get("dec_far")))
    step("enc_two", lambda: add32(enc_of("_two", near(0)), get("enc_far")))
    for kind in ("dec", "enc"):
        send(kind + "_up", functools.partial(get, kind + "_two"), "lat", up_two)
        send(kind + "_down", functools.partial(get, kind + "_two"), "lat", down_two)
    send("dec_prev", lambda: add32(dec_of(jnp.minimum(z + 1, 3)), get("dec_up")), "lat", up)
    send("dec_next", lambda: add32(dec_of(jnp.maximum(z - 1, 0)), get("dec_down")), "lat", down)
    send("enc_prev", lambda: add32(enc_of("_near", near(1)), get("enc_up")), "lat", up)
    send("enc_next", lambda: add32(enc_of("_near", near(2)), get("enc_down")), "lat", down)
    step("dec_own", lambda: dec_of(z))
    step("enc_own", lambda: enc_of("_near", near(0)))

    def total(kind):
        value = get(kind + "_own") + get(kind + "_prev").astype(jnp.float32) + get(kind + "_next").astype(jnp.float32)
        return value.astype(jnp.bfloat16)

    return total("dec")[:, None, :], total("enc").T[None]


def shards_any(acts, err_grad, codes, dec_weight, act_ids, act_count):
    z = lax.axis_index("lat")
    x = lax.axis_index("tok")
    rows = err_grad.shape[1]
    lat = dec_weight.shape[0]
    width = acts.shape[3]
    groups = acts.shape[0]
    blocks = lax.axis_size("lat")
    w_own = lax.dynamic_slice_in_dim(dec_weight.reshape(lat, -1), x * width, width, 1)
    w_all = lax.all_gather(w_own, "lat", axis=0, tiled=True)
    err = lax.all_to_all(err_grad, "tok", split_axis=3, concat_axis=0, tiled=True)
    err = err.reshape(groups * rows, width)
    ids = valid_ids(act_ids, act_count)
    code_hits = row_hits(lax.dynamic_slice_in_dim(ids, x, 1, 0), 0, codes.shape[1], z)
    used = codes[0] * code_hits.astype(jnp.bfloat16).T
    used = lax.all_to_all(used, "lat", split_axis=0, concat_axis=1, tiled=True)
    used = lax.all_gather(used, "tok", axis=0, tiled=True)
    dec_part = dot32(used, err, CONTRACT_ROWS)
    grad_dec = lax.psum_scatter(dec_part, "lat", scatter_dimension=0, tiled=True)
    dlat = lax.psum(dot32(err, w_all, CONTRACT_LAST), ("tok", "sub"))
    hits = [row_hits(ids, z * rows, rows, block).reshape(groups * rows, 1) for block in range(blocks)]
    hits = jnp.concatenate([jnp.broadcast_to(h, (groups * rows, lat)) for h in hits], axis=1)
    dcodes = (dlat * hits).astype(jnp.bfloat16)
    enc_part = dot32(acts.reshape(groups * rows, width), dcodes, CONTRACT_ROWS)
    grad_enc = lax.psum_scatter(enc_part, "lat", scatter_dimension=1, tiled=True)
    return grad_dec.astype(jnp.bfloat16)[:, None, :], grad_enc.astype(jnp.bfloat16)[None]


def solution(mesh):
    line = mesh.shape["lat"] == 4 and mesh.shape["tok"] == 2
    return jax.shard_map(
        shards_line if line else shards_any,
        mesh=mesh,
        in_specs=(
            P("groups", "lat", "sub", "tok"),
            P(("groups", "tok"), "lat", "sub", None),
            P(("groups", "tok"), None, "lat"),
            P(("groups", "lat"), "sub", None),
            P("groups", None, None),
            P("groups", None),
        ),
        out_specs=(P(("groups", "lat"), "sub", "tok"), P("sub", "tok", ("groups", "lat"))),
        check_vma=False,
    )
```

```python
import functools

import jax
import jax.numpy as jnp
from jax import lax
from jax.experimental import pallas as pl
from jax.experimental.pallas import tpu as pltpu
from jax.sharding import PartitionSpec as P

TBLK = 256
ORDER = {
    "w_3": ("dec",),
    "w_3_in": ("codes",),
    "sub_near": ("dec_far",),
    "w_2": ("enc_far_in",),
    "tok_two": ("dec_pair_in", "dec_last_in",),
    "enc_mid": ("dec_pair",),
}
CONTRACT_LAST = (((1,), (1,)), ((), ()))
PLAIN = (((1,), (0,)), ((), ()))
CONTRACT_ROWS = (((0,), (0,)), ((), ()))


def dot32(left, right, dims):
    return lax.dot_general(left, right, dims, preferred_element_type=jnp.float32)


def local_call(body, out_shape, scalars, *args):
    vmem = pl.BlockSpec(memory_space=pltpu.VMEM)
    return pl.pallas_call(
        body,
        out_shape=out_shape,
        in_specs=[pl.BlockSpec(memory_space=pltpu.SMEM)] + [vmem] * len(args),
        out_specs=jax.tree.map(lambda _: vmem, out_shape),
        compiler_params=pltpu.CompilerParams(vmem_limit_bytes=32 * 2**20),
        cost_estimate=pl.CostEstimate(flops=0, bytes_accessed=0, transcendentals=0),
    )(jnp.stack(scalars).astype(jnp.int32), *args)


def turned(value):
    return value.astype(jnp.float32).T.astype(jnp.bfloat16)


def dec_body(block_ref, own_ref, other_ref, err_own_ref, err_other_ref, *out_refs):
    block = block_ref[0]
    total = dot32(turned(own_ref[block]), err_own_ref[...], PLAIN)
    total += dot32(turned(other_ref[block]), err_other_ref[...], PLAIN)
    for out_ref in out_refs:
        out_ref[...] = total.astype(out_ref.dtype)


def dlat_body(place_ref, own_ref, other_ref, *refs):
    place, out_ref = place_ref[0], refs[-1]
    for i, w_ref in enumerate(refs[:-1]):
        lanes = slice(i * w_ref.shape[0], (i + 1) * w_ref.shape[0])
        out_ref[place, :, lanes] = dot32(own_ref[...], w_ref[...], CONTRACT_LAST)
        out_ref[1 - place, :, lanes] = dot32(other_ref[...], w_ref[...], CONTRACT_LAST)


def enc_body(core_ref, acts_ref, mine_ref, other_ref, out_ref):
    core = core_ref[0]
    total = dot32(turned(mine_ref[...]), acts_ref[core], PLAIN)
    total += dot32(turned(other_ref[...]), acts_ref[1 - core], PLAIN)
    out_ref[...] = total.astype(out_ref.dtype)


def valid_ids(act_ids, act_count):
    slot = jnp.arange(act_ids.shape[2], dtype=jnp.int32)
    return jnp.where(slot[None, None, :] < act_count[:, :, None], act_ids, -1)


def row_hits(ids, first_row, rows, block):
    on = jnp.any(ids == block, axis=2)
    tile = (first_row + jnp.arange(rows, dtype=jnp.int32)) // TBLK
    hit = on[:, :, None] & (tile[None, None, :] == jnp.arange(ids.shape[1])[None, :, None])
    return jnp.any(hit, axis=1).astype(jnp.float32)


def shards_line(acts, err_grad, codes, dec_weight, act_ids, act_count):
    z = lax.axis_index("lat")
    x = lax.axis_index("tok")
    c = lax.axis_index("sub")
    rows = err_grad.shape[1]
    lat = dec_weight.shape[0]
    width = acts.shape[3]
    swap = [(0, 1), (1, 0)]
    pairs = [(0, 1), (1, 0), (2, 3), (3, 2)]
    inward, outward, across, ends = [(0, 1), (3, 2)], [(1, 0), (2, 3)], [(1, 2), (2, 1)], [(0, 3), (3, 0)]
    at_end = (z == 0) | (z == 3)

    ids = valid_ids(act_ids, act_count)
    act_rows = acts.reshape(2, rows, width)
    err_rows = err_grad.reshape(rows, -1)
    block = jax.ShapeDtypeStruct((lat, width), jnp.float32)
    block16 = jax.ShapeDtypeStruct((lat, width), jnp.bfloat16)
    steps, done = {}, {}

    def get(name):
        if name not in done:
            value = steps[name]()
            others = [get(other) for other in ORDER.get(name, ())]
            done[name] = lax.optimization_barrier((value, *others))[0] if others else value
        return done[name]

    def step(name, make):
        steps[name] = make

    def send(name, source, axis, pairs):
        step(name + "_in", source)
        step(name, lambda: lax.ppermute(get(name + "_in"), axis, pairs))

    def add32(term, got):
        return (term + got.astype(jnp.float32)).astype(jnp.bfloat16)

    step("weights", lambda: dec_weight.reshape(lat, -1))
    step("w_own", lambda: lax.dynamic_slice_in_dim(get("weights"), x * width, width, 1))
    send("w_1", lambda: get("w_own"), "lat", pairs)
    send("w_3", lambda: get("w_own"), "lat", across + ends)

    step("err_own", lambda: lax.dynamic_slice_in_dim(err_rows, x * width, width, 1))
    send("err", lambda: lax.dynamic_slice_in_dim(err_rows, (1 - x) * width, width, 1), "tok", swap)

    step("codes_in", lambda: codes.reshape(4, rows, lat))
    step("codes", lambda: lax.all_to_all(get("codes_in"), "lat", split_axis=0, concat_axis=0, tiled=True))
    send("codes_other", lambda: get("codes"), "tok", swap)

    def used(value, group):
        all_hits = jnp.stack([row_hits(ids, z * rows, rows, b) for b in range(4)])
        hit = lax.dynamic_index_in_dim(all_hits, group, 1, keepdims=False)
        return value * hit[:, :, None].astype(jnp.bfloat16)

    step("used_own", lambda: used(get("codes"), x))
    step("used_other", lambda: used(get("codes_other"), 1 - x))

    def dec_of(b, *out):
        codes_pair = get("used_own"), get("used_other")
        return local_call(dec_body, out, [b], *codes_pair, get("err_own"), get("err"))

    step("dec", lambda: dec_of(z ^ 3, block16))

    send("w_across", lambda: get("w_1"), "lat", across)
    send("w_out", lambda: get("w_3"), "lat", outward)
    send("dec_far", lambda: get("dec")[0], "lat", inward)
    step("w_2", lambda: jnp.where(at_end, get("w_out"), get("w_across")))

    def latent_grads(tag, names, blocks):
        def part():
            weights = [get(name) for name in names]
            out = jax.ShapeDtypeStruct((2, rows, lat * len(weights)), jnp.float32)
            return local_call(dlat_body, out, [c ^ x], get("err_own"), get("err"), *weights)

        def mine():
            total, cols = get("sums" + tag) + get("tok" + tag), []
            for i, b in enumerate(blocks):
                hit = lax.dynamic_index_in_dim(row_hits(ids, z * rows, rows, b), c, 0, keepdims=False)
                cols.append((total[:, i * lat : (i + 1) * lat] * hit[:, None]).astype(jnp.bfloat16))
            return jnp.concatenate(cols, axis=1)

        step("part" + tag, part)
        send("sub" + tag, lambda: get("part" + tag)[1], "sub", swap)
        step("sums" + tag, lambda: get("part" + tag)[0] + get("sub" + tag))
        send("tok" + tag, lambda: get("sums" + tag), "tok", swap)
        step("mine" + tag, mine)
        send("other" + tag, lambda: get("mine" + tag), "sub", swap)

    latent_grads("_near", ["w_own", "w_1", "w_3"], [z, z ^ 1, z ^ 3])
    latent_grads("_two", ["w_2"], [z ^ 2])

    def enc_of(tag, pick, out=block):
        return local_call(enc_body, out, [c], act_rows, pick(get("mine" + tag)), pick(get("other" + tag)))

    def near(i):
        return lambda part: part[:, i * lat : (i + 1) * lat]

    send("enc_far", lambda: enc_of("_near", near(2), block16), "lat", inward)
    step("enc_own", lambda: enc_of("_near", near(0)))
    step("enc_1", lambda: enc_of("_near", near(1)))
    step("enc_2", lambda: enc_of("_two", near(0)))
    step("enc_3", lambda: enc_of("_near", near(2)))
    for j, name in enumerate(("dec_own", "dec_1", "dec_2", "dec_3")):
        step(name, lambda j=j: dec_of(z ^ j, block)[0])

    def line_sums(kind):
        step(kind + "_two", lambda: add32(get(kind + "_2"), get(kind + "_far")))
        send(kind + "_in", lambda: get(kind + "_two"), "lat", inward)
        send(kind + "_mid", lambda: get(kind + "_two"), "lat", across)
        send(kind + "_pair", lambda: add32(get(kind + "_1"), get(kind + "_mid")), "lat", pairs)
        send(kind + "_last", lambda: add32(get(kind + "_3"), get(kind + "_in")), "lat", across)

    line_sums("dec")
    line_sums("enc")

    def total(kind):
        value = get(kind + "_own") + get(kind + "_pair").astype(jnp.float32) + get(kind + "_last").astype(jnp.float32)
        return value.astype(jnp.bfloat16)

    return total("dec")[:, None, :], total("enc").T[None]


def shards_any(acts, err_grad, codes, dec_weight, act_ids, act_count):
    z = lax.axis_index("lat")
    x = lax.axis_index("tok")
    rows = err_grad.shape[1]
    lat = dec_weight.shape[0]
    width = acts.shape[3]
    groups = acts.shape[0]
    blocks = lax.axis_size("lat")
    w_own = lax.dynamic_slice_in_dim(dec_weight.reshape(lat, -1), x * width, width, 1)
    w_all = lax.all_gather(w_own, "lat", axis=0, tiled=True)
    err = lax.all_to_all(err_grad, "tok", split_axis=3, concat_axis=0, tiled=True)
    err = err.reshape(groups * rows, width)
    ids = valid_ids(act_ids, act_count)
    code_hits = row_hits(lax.dynamic_slice_in_dim(ids, x, 1, 0), 0, codes.shape[1], z)
    used = codes[0] * code_hits.astype(jnp.bfloat16).T
    used = lax.all_to_all(used, "lat", split_axis=0, concat_axis=1, tiled=True)
    used = lax.all_gather(used, "tok", axis=0, tiled=True)
    dec_part = dot32(used, err, CONTRACT_ROWS)
    grad_dec = lax.psum_scatter(dec_part, "lat", scatter_dimension=0, tiled=True)
    dlat = lax.psum(dot32(err, w_all, CONTRACT_LAST), ("tok", "sub"))
    hits = [row_hits(ids, z * rows, rows, block).reshape(groups * rows, 1) for block in range(blocks)]
    hits = jnp.concatenate([jnp.broadcast_to(h, (groups * rows, lat)) for h in hits], axis=1)
    dcodes = (dlat * hits).astype(jnp.bfloat16)
    enc_part = dot32(acts.reshape(groups * rows, width), dcodes, CONTRACT_ROWS)
    grad_enc = lax.psum_scatter(enc_part, "lat", scatter_dimension=1, tiled=True)
    return grad_dec.astype(jnp.bfloat16)[:, None, :], grad_enc.astype(jnp.bfloat16)[None]


def solution(mesh):
    line = mesh.shape["lat"] == 4 and mesh.shape["tok"] == 2
    return jax.shard_map(
        shards_line if line else shards_any,
        mesh=mesh,
        in_specs=(
            P("groups", "lat", "sub", "tok"),
            P(("groups", "tok"), "lat", "sub", None),
            P(("groups", "tok"), None, "lat"),
            P(("groups", "lat"), "sub", None),
            P("groups", None, None),
            P("groups", None),
        ),
        out_specs=(P(("groups", "lat"), "sub", "tok"), P("sub", "tok", ("groups", "lat"))),
        check_vma=False,
    )
```

```python
import functools

import jax
import jax.numpy as jnp
from jax import lax
from jax.experimental import pallas as pl
from jax.experimental.pallas import tpu as pltpu
from jax.sharding import PartitionSpec as P

TBLK = 256
ORDER = {
    "w_far_in": ("codes",),
    "w_mid_in": ("codes",),
    "w_far": ("dec",),
    "sub_near": ("dec_far",),
    "tok_near_in": ("dec_far",),
    "w_2": ("enc_far_in",),
    "tok_rest": ("dec_pair_in", "dec_last_in",),
    "enc_mid": ("dec_pair",),
}
CONTRACT_LAST = (((1,), (1,)), ((), ()))
PLAIN = (((1,), (0,)), ((), ()))
CONTRACT_ROWS = (((0,), (0,)), ((), ()))


def dot32(left, right, dims):
    return lax.dot_general(left, right, dims, preferred_element_type=jnp.float32)


def local_call(body, out_shape, scalars, *args):
    vmem = pl.BlockSpec(memory_space=pltpu.VMEM)
    return pl.pallas_call(
        body,
        out_shape=out_shape,
        in_specs=[pl.BlockSpec(memory_space=pltpu.SMEM)] + [vmem] * len(args),
        out_specs=jax.tree.map(lambda _: vmem, out_shape),
        compiler_params=pltpu.CompilerParams(vmem_limit_bytes=32 * 2**20),
        cost_estimate=pl.CostEstimate(flops=0, bytes_accessed=0, transcendentals=0),
    )(jnp.stack(scalars).astype(jnp.int32), *args)


def turned(value):
    return value.astype(jnp.float32).T.astype(jnp.bfloat16)


def dec_body(block_ref, own_ref, other_ref, err_own_ref, err_other_ref, *out_refs):
    block = block_ref[0]
    total = dot32(turned(own_ref[block]), err_own_ref[...], PLAIN)
    total += dot32(turned(other_ref[block]), err_other_ref[...], PLAIN)
    for out_ref in out_refs:
        out_ref[...] = total.astype(out_ref.dtype)


def dlat_body(place_ref, own_ref, other_ref, *refs):
    place, out_ref = place_ref[0], refs[-1]
    for i, w_ref in enumerate(refs[:-1]):
        lanes = slice(i * w_ref.shape[0], (i + 1) * w_ref.shape[0])
        out_ref[place, :, lanes] = dot32(own_ref[...], w_ref[...], CONTRACT_LAST)
        out_ref[1 - place, :, lanes] = dot32(other_ref[...], w_ref[...], CONTRACT_LAST)


def enc_body(core_ref, acts_ref, mine_ref, other_ref, out_ref):
    core = core_ref[0]
    total = dot32(turned(mine_ref[...]), acts_ref[core], PLAIN)
    total += dot32(turned(other_ref[...]), acts_ref[1 - core], PLAIN)
    out_ref[...] = total.astype(out_ref.dtype)


def valid_ids(act_ids, act_count):
    slot = jnp.arange(act_ids.shape[2], dtype=jnp.int32)
    return jnp.where(slot[None, None, :] < act_count[:, :, None], act_ids, -1)


def row_hits(ids, first_row, rows, block):
    on = jnp.any(ids == block, axis=2)
    tile = (first_row + jnp.arange(rows, dtype=jnp.int32)) // TBLK
    hit = on[:, :, None] & (tile[None, None, :] == jnp.arange(ids.shape[1])[None, :, None])
    return jnp.any(hit, axis=1).astype(jnp.float32)


def shards_line(acts, err_grad, codes, dec_weight, act_ids, act_count):
    z = lax.axis_index("lat")
    x = lax.axis_index("tok")
    c = lax.axis_index("sub")
    rows = err_grad.shape[1]
    lat = dec_weight.shape[0]
    width = acts.shape[3]
    swap = [(0, 1), (1, 0)]
    pairs = [(0, 1), (1, 0), (2, 3), (3, 2)]
    inward, outward, across, ends = [(0, 1), (3, 2)], [(1, 0), (2, 3)], [(1, 2), (2, 1)], [(0, 3), (3, 0)]
    at_end = (z == 0) | (z == 3)

    ids = valid_ids(act_ids, act_count)
    act_rows = acts.reshape(2, rows, width)
    err_rows = err_grad.reshape(rows, -1)
    block = jax.ShapeDtypeStruct((lat, width), jnp.float32)
    block16 = jax.ShapeDtypeStruct((lat, width), jnp.bfloat16)
    steps, done = {}, {}

    def get(name):
        if name not in done:
            value = steps[name]()
            others = [get(other) for other in ORDER.get(name, ())]
            done[name] = lax.optimization_barrier((value, *others))[0] if others else value
        return done[name]

    def step(name, make):
        steps[name] = make

    def send(name, source, axis, pairs):
        step(name + "_in", source)
        step(name, lambda: lax.ppermute(get(name + "_in"), axis, pairs))

    def add32(term, got):
        return (term + got.astype(jnp.float32)).astype(jnp.bfloat16)

    step("weights", lambda: dec_weight.reshape(lat, -1))
    step("w_own", lambda: lax.dynamic_slice_in_dim(get("weights"), x * width, width, 1))
    send("w_1", lambda: get("w_own"), "lat", pairs)
    send("w_far", lambda: get("w_own"), "lat", ends)
    send("w_mid", lambda: get("w_own"), "lat", across)

    step("err_own", lambda: lax.dynamic_slice_in_dim(err_rows, x * width, width, 1))
    send("err", lambda: lax.dynamic_slice_in_dim(err_rows, (1 - x) * width, width, 1), "tok", swap)

    step("codes_in", lambda: codes.reshape(4, rows, lat))
    step("codes", lambda: lax.all_to_all(get("codes_in"), "lat", split_axis=0, concat_axis=0, tiled=True))
    send("codes_other", lambda: get("codes"), "tok", swap)

    def used(value, group):
        all_hits = jnp.stack([row_hits(ids, z * rows, rows, b) for b in range(4)])
        hit = lax.dynamic_index_in_dim(all_hits, group, 1, keepdims=False)
        return value * hit[:, :, None].astype(jnp.bfloat16)

    step("used_own", lambda: used(get("codes"), x))
    step("used_other", lambda: used(get("codes_other"), 1 - x))

    def dec_of(b, *out):
        codes_pair = get("used_own"), get("used_other")
        return local_call(dec_body, out, [b], *codes_pair, get("err_own"), get("err"))

    step("dec", lambda: dec_of(z ^ 3, block16))

    send("w_across", lambda: get("w_1"), "lat", across)
    send("w_out", lambda: get("w_mid"), "lat", outward)
    send("dec_far", lambda: get("dec")[0], "lat", inward)
    step("w_2", lambda: jnp.where(at_end, get("w_out"), get("w_across")))

    def latent_grads(tag, names, blocks):
        def part():
            weights = [get(name) for name in names]
            out = jax.ShapeDtypeStruct((2, rows, lat * len(weights)), jnp.float32)
            return local_call(dlat_body, out, [c ^ x], get("err_own"), get("err"), *weights)

        def mine():
            total, cols = get("sums" + tag) + get("tok" + tag), []
            for i, b in enumerate(blocks):
                hit = lax.dynamic_index_in_dim(row_hits(ids, z * rows, rows, b), c, 0, keepdims=False)
                cols.append((total[:, i * lat : (i + 1) * lat] * hit[:, None]).astype(jnp.bfloat16))
            return jnp.concatenate(cols, axis=1)

        step("part" + tag, part)
        send("sub" + tag, lambda: get("part" + tag)[1], "sub", swap)
        step("sums" + tag, lambda: get("part" + tag)[0] + get("sub" + tag))
        send("tok" + tag, lambda: get("sums" + tag), "tok", swap)
        step("mine" + tag, mine)
        send("other" + tag, lambda: get("mine" + tag), "sub", swap)

    latent_grads("_near", ["w_own", "w_far"], [z, z ^ 3])
    latent_grads("_rest", ["w_2", "w_mid", "w_1"], [z ^ 2, z ^ 3, z ^ 1])

    def enc_of(tag, pick, out=block):
        return local_call(enc_body, out, [c], act_rows, pick(get("mine" + tag)), pick(get("other" + tag)))

    def cols_of(i):
        return lambda part: part[:, i * lat : (i + 1) * lat]

    send("enc_far", lambda: enc_of("_near", cols_of(1), block16), "lat", inward)
    step("enc_own", lambda: enc_of("_near", cols_of(0)))
    step("enc_1", lambda: enc_of("_rest", cols_of(2)))
    step("enc_2", lambda: enc_of("_rest", cols_of(0)))
    step("enc_3", lambda: enc_of("_rest", cols_of(1)))
    for j, name in enumerate(("dec_own", "dec_1", "dec_2", "dec_3")):
        step(name, lambda j=j: dec_of(z ^ j, block)[0])

    def line_sums(kind):
        step(kind + "_two", lambda: add32(get(kind + "_2"), get(kind + "_far")))
        send(kind + "_in", lambda: get(kind + "_two"), "lat", inward)
        send(kind + "_mid", lambda: get(kind + "_two"), "lat", across)
        send(kind + "_pair", lambda: add32(get(kind + "_1"), get(kind + "_mid")), "lat", pairs)
        send(kind + "_last", lambda: add32(get(kind + "_3"), get(kind + "_in")), "lat", across)

    line_sums("dec")
    line_sums("enc")

    def total(kind):
        value = get(kind + "_own") + get(kind + "_pair").astype(jnp.float32) + get(kind + "_last").astype(jnp.float32)
        return value.astype(jnp.bfloat16)

    return total("dec")[:, None, :], total("enc").T[None]


def shards_any(acts, err_grad, codes, dec_weight, act_ids, act_count):
    z = lax.axis_index("lat")
    x = lax.axis_index("tok")
    rows = err_grad.shape[1]
    lat = dec_weight.shape[0]
    width = acts.shape[3]
    groups = acts.shape[0]
    blocks = lax.axis_size("lat")
    w_own = lax.dynamic_slice_in_dim(dec_weight.reshape(lat, -1), x * width, width, 1)
    w_all = lax.all_gather(w_own, "lat", axis=0, tiled=True)
    err = lax.all_to_all(err_grad, "tok", split_axis=3, concat_axis=0, tiled=True)
    err = err.reshape(groups * rows, width)
    ids = valid_ids(act_ids, act_count)
    code_hits = row_hits(lax.dynamic_slice_in_dim(ids, x, 1, 0), 0, codes.shape[1], z)
    used = codes[0] * code_hits.astype(jnp.bfloat16).T
    used = lax.all_to_all(used, "lat", split_axis=0, concat_axis=1, tiled=True)
    used = lax.all_gather(used, "tok", axis=0, tiled=True)
    dec_part = dot32(used, err, CONTRACT_ROWS)
    grad_dec = lax.psum_scatter(dec_part, "lat", scatter_dimension=0, tiled=True)
    dlat = lax.psum(dot32(err, w_all, CONTRACT_LAST), ("tok", "sub"))
    hits = [row_hits(ids, z * rows, rows, block).reshape(groups * rows, 1) for block in range(blocks)]
    hits = jnp.concatenate([jnp.broadcast_to(h, (groups * rows, lat)) for h in hits], axis=1)
    dcodes = (dlat * hits).astype(jnp.bfloat16)
    enc_part = dot32(acts.reshape(groups * rows, width), dcodes, CONTRACT_ROWS)
    grad_enc = lax.psum_scatter(enc_part, "lat", scatter_dimension=1, tiled=True)
    return grad_dec.astype(jnp.bfloat16)[:, None, :], grad_enc.astype(jnp.bfloat16)[None]


def solution(mesh):
    line = mesh.shape["lat"] == 4 and mesh.shape["tok"] == 2
    return jax.shard_map(
        shards_line if line else shards_any,
        mesh=mesh,
        in_specs=(
            P("groups", "lat", "sub", "tok"),
            P(("groups", "tok"), "lat", "sub", None),
            P(("groups", "tok"), None, "lat"),
            P(("groups", "lat"), "sub", None),
            P("groups", None, None),
            P("groups", None),
        ),
        out_specs=(P(("groups", "lat"), "sub", "tok"), P("sub", "tok", ("groups", "lat"))),
        check_vma=False,
    )
```

```python
import functools

import jax
import jax.numpy as jnp
from jax import lax
from jax.experimental import pallas as pl
from jax.experimental.pallas import tpu as pltpu
from jax.sharding import PartitionSpec as P

TBLK = 256
ORDER = {
    "w_far_in": ("codes",),
    "w_mid_in": ("codes",),
    "w_far": ("dec",),
    "sub_near": ("dec_far",),
    "tok_near_in": ("dec_far",),
    "w_2": ("enc_far_in",),
    "tok_rest": ("dec_pair_in", "dec_last_in",),
    "enc_mid": ("dec_pair",),
    "sub_rest": ("dec_two",),
    "w_across": ("tok_near", "w_out",),
}
CONTRACT_LAST = (((1,), (1,)), ((), ()))
PLAIN = (((1,), (0,)), ((), ()))
CONTRACT_ROWS = (((0,), (0,)), ((), ()))


def dot32(left, right, dims):
    return lax.dot_general(left, right, dims, preferred_element_type=jnp.float32)


def local_call(body, out_shape, scalars, *args):
    vmem = pl.BlockSpec(memory_space=pltpu.VMEM)
    return pl.pallas_call(
        body,
        out_shape=out_shape,
        in_specs=[pl.BlockSpec(memory_space=pltpu.SMEM)] + [vmem] * len(args),
        out_specs=jax.tree.map(lambda _: vmem, out_shape),
        compiler_params=pltpu.CompilerParams(vmem_limit_bytes=12 * 2**20),
        cost_estimate=pl.CostEstimate(flops=0, bytes_accessed=0, transcendentals=0),
    )(jnp.stack(scalars).astype(jnp.int32), *args)


def turned(value):
    return value.astype(jnp.float32).T.astype(jnp.bfloat16)


def dec_body(block_ref, own_ref, other_ref, err_own_ref, err_other_ref, *out_refs):
    block = block_ref[0]
    total = dot32(turned(own_ref[block]), err_own_ref[...], PLAIN)
    total += dot32(turned(other_ref[block]), err_other_ref[...], PLAIN)
    for out_ref in out_refs:
        out_ref[...] = total.astype(out_ref.dtype)


def dlat_body(place_ref, own_ref, other_ref, *refs):
    place, out_ref = place_ref[0], refs[-1]
    for i, w_ref in enumerate(refs[:-1]):
        lanes = slice(i * w_ref.shape[0], (i + 1) * w_ref.shape[0])
        out_ref[place, :, lanes] = dot32(own_ref[...], w_ref[...], CONTRACT_LAST)
        out_ref[1 - place, :, lanes] = dot32(other_ref[...], w_ref[...], CONTRACT_LAST)


def enc_body(core_ref, acts_ref, mine_ref, other_ref, out_ref):
    core = core_ref[0]
    total = dot32(turned(mine_ref[...]), acts_ref[core], PLAIN)
    total += dot32(turned(other_ref[...]), acts_ref[1 - core], PLAIN)
    out_ref[...] = total.astype(out_ref.dtype)


def valid_ids(act_ids, act_count):
    slot = jnp.arange(act_ids.shape[2], dtype=jnp.int32)
    return jnp.where(slot[None, None, :] < act_count[:, :, None], act_ids, -1)


def row_hits(ids, first_row, rows, block):
    on = jnp.any(ids == block, axis=2)
    tile = (first_row + jnp.arange(rows, dtype=jnp.int32)) // TBLK
    hit = on[:, :, None] & (tile[None, None, :] == jnp.arange(ids.shape[1])[None, :, None])
    return jnp.any(hit, axis=1).astype(jnp.float32)


def shards_line(acts, err_grad, codes, dec_weight, act_ids, act_count):
    z = lax.axis_index("lat")
    x = lax.axis_index("tok")
    c = lax.axis_index("sub")
    rows = err_grad.shape[1]
    lat = dec_weight.shape[0]
    width = acts.shape[3]
    swap = [(0, 1), (1, 0)]
    pairs = [(0, 1), (1, 0), (2, 3), (3, 2)]
    inward, outward, across, ends = [(0, 1), (3, 2)], [(1, 0), (2, 3)], [(1, 2), (2, 1)], [(0, 3), (3, 0)]
    at_end = (z == 0) | (z == 3)

    ids = valid_ids(act_ids, act_count)
    act_rows = acts.reshape(2, rows, width)
    err_rows = err_grad.reshape(rows, -1)
    block = jax.ShapeDtypeStruct((lat, width), jnp.float32)
    block16 = jax.ShapeDtypeStruct((lat, width), jnp.bfloat16)
    steps, done = {}, {}

    def get(name):
        if name not in done:
            value = steps[name]()
            others = [get(other) for other in ORDER.get(name, ())]
            done[name] = lax.optimization_barrier((value, *others))[0] if others else value
        return done[name]

    def step(name, make):
        steps[name] = make

    def send(name, source, axis, pairs):
        step(name + "_in", source)
        step(name, lambda: lax.ppermute(get(name + "_in"), axis, pairs))

    def add32(term, got):
        return (term + got.astype(jnp.float32)).astype(jnp.bfloat16)

    step("weights", lambda: dec_weight.reshape(lat, -1))
    step("w_own", lambda: lax.dynamic_slice_in_dim(get("weights"), x * width, width, 1))
    send("w_1", lambda: get("w_own"), "lat", pairs)
    send("w_far", lambda: get("w_own"), "lat", ends)
    send("w_mid", lambda: get("w_own"), "lat", across)

    step("err_own", lambda: lax.dynamic_slice_in_dim(err_rows, x * width, width, 1))
    send("err", lambda: lax.dynamic_slice_in_dim(err_rows, (1 - x) * width, width, 1), "tok", swap)

    step("codes_in", lambda: codes.reshape(4, rows, lat))
    step("codes", lambda: lax.all_to_all(get("codes_in"), "lat", split_axis=0, concat_axis=0, tiled=True))
    send("codes_other", lambda: get("codes"), "tok", swap)

    def used(value, group):
        all_hits = jnp.stack([row_hits(ids, z * rows, rows, b) for b in range(4)])
        hit = lax.dynamic_index_in_dim(all_hits, group, 1, keepdims=False)
        return value * hit[:, :, None].astype(jnp.bfloat16)

    step("used_own", lambda: used(get("codes"), x))
    step("used_other", lambda: used(get("codes_other"), 1 - x))

    def dec_of(b, *out):
        codes_pair = get("used_own"), get("used_other")
        return local_call(dec_body, out, [b], *codes_pair, get("err_own"), get("err"))

    step("dec", lambda: dec_of(z ^ 3, block16))

    send("w_across", lambda: get("w_1"), "lat", across)
    send("w_out", lambda: get("w_mid"), "lat", outward)
    send("dec_far", lambda: get("dec")[0], "lat", inward)
    step("w_2", lambda: jnp.where(at_end, get("w_out"), get("w_across")))

    def latent_grads(tag, names, blocks):
        def part():
            weights = [get(name) for name in names]
            out = jax.ShapeDtypeStruct((2, rows, lat * len(weights)), jnp.float32)
            return local_call(dlat_body, out, [c ^ x], get("err_own"), get("err"), *weights)

        def mine():
            total, cols = get("sums" + tag) + get("tok" + tag), []
            for i, b in enumerate(blocks):
                hit = lax.dynamic_index_in_dim(row_hits(ids, z * rows, rows, b), c, 0, keepdims=False)
                cols.append((total[:, i * lat : (i + 1) * lat] * hit[:, None]).astype(jnp.bfloat16))
            return jnp.concatenate(cols, axis=1)

        step("part" + tag, part)
        send("sub" + tag, lambda: get("part" + tag)[1], "sub", swap)
        step("sums" + tag, lambda: get("part" + tag)[0] + get("sub" + tag))
        send("tok" + tag, lambda: get("sums" + tag), "tok", swap)
        step("mine" + tag, mine)
        send("other" + tag, lambda: get("mine" + tag), "sub", swap)

    latent_grads("_near", ["w_own", "w_far"], [z, z ^ 3])
    latent_grads("_rest", ["w_2", "w_mid", "w_1"], [z ^ 2, z ^ 3, z ^ 1])

    def enc_of(tag, pick, out=block):
        return local_call(enc_body, out, [c], act_rows, pick(get("mine" + tag)), pick(get("other" + tag)))

    def cols_of(i):
        return lambda part: part[:, i * lat : (i + 1) * lat]

    send("enc_far", lambda: enc_of("_near", cols_of(1), block16), "lat", inward)
    step("enc_own", lambda: enc_of("_near", cols_of(0)))
    step("enc_1", lambda: enc_of("_rest", cols_of(2)))
    step("enc_2", lambda: enc_of("_rest", cols_of(0)))
    step("enc_3", lambda: enc_of("_rest", cols_of(1)))
    for j, name in enumerate(("dec_own", "dec_1", "dec_2", "dec_3")):
        step(name, lambda j=j: dec_of(z ^ j, block)[0])

    def line_sums(kind):
        step(kind + "_two", lambda: add32(get(kind + "_2"), get(kind + "_far")))
        send(kind + "_in", lambda: get(kind + "_2").astype(jnp.bfloat16), "lat", inward)
        send(kind + "_mid", lambda: get(kind + "_two"), "lat", across)
        send(kind + "_pair", lambda: add32(get(kind + "_1"), get(kind + "_mid")), "lat", pairs)
        send(kind + "_last", lambda: add32(get(kind + "_3"), get(kind + "_in")), "lat", across)

    line_sums("dec")
    line_sums("enc")

    def total(kind):
        value = get(kind + "_own") + get(kind + "_pair").astype(jnp.float32) + get(kind + "_last").astype(jnp.float32)
        return value.astype(jnp.bfloat16)

    return total("dec")[:, None, :], total("enc").T[None]


def shards_any(acts, err_grad, codes, dec_weight, act_ids, act_count):
    z = lax.axis_index("lat")
    x = lax.axis_index("tok")
    rows = err_grad.shape[1]
    lat = dec_weight.shape[0]
    width = acts.shape[3]
    groups = acts.shape[0]
    blocks = lax.axis_size("lat")
    w_own = lax.dynamic_slice_in_dim(dec_weight.reshape(lat, -1), x * width, width, 1)
    w_all = lax.all_gather(w_own, "lat", axis=0, tiled=True)
    err = lax.all_to_all(err_grad, "tok", split_axis=3, concat_axis=0, tiled=True)
    err = err.reshape(groups * rows, width)
    ids = valid_ids(act_ids, act_count)
    code_hits = row_hits(lax.dynamic_slice_in_dim(ids, x, 1, 0), 0, codes.shape[1], z)
    used = codes[0] * code_hits.astype(jnp.bfloat16).T
    used = lax.all_to_all(used, "lat", split_axis=0, concat_axis=1, tiled=True)
    used = lax.all_gather(used, "tok", axis=0, tiled=True)
    dec_part = dot32(used, err, CONTRACT_ROWS)
    grad_dec = lax.psum_scatter(dec_part, "lat", scatter_dimension=0, tiled=True)
    dlat = lax.psum(dot32(err, w_all, CONTRACT_LAST), ("tok", "sub"))
    hits = [row_hits(ids, z * rows, rows, block).reshape(groups * rows, 1) for block in range(blocks)]
    hits = jnp.concatenate([jnp.broadcast_to(h, (groups * rows, lat)) for h in hits], axis=1)
    dcodes = (dlat * hits).astype(jnp.bfloat16)
    enc_part = dot32(acts.reshape(groups * rows, width), dcodes, CONTRACT_ROWS)
    grad_enc = lax.psum_scatter(enc_part, "lat", scatter_dimension=1, tiled=True)
    return grad_dec.astype(jnp.bfloat16)[:, None, :], grad_enc.astype(jnp.bfloat16)[None]


def solution(mesh):
    line = mesh.shape["lat"] == 4 and mesh.shape["tok"] == 2
    return jax.shard_map(
        shards_line if line else shards_any,
        mesh=mesh,
        in_specs=(
            P("groups", "lat", "sub", "tok"),
            P(("groups", "tok"), "lat", "sub", None),
            P(("groups", "tok"), None, "lat"),
            P(("groups", "lat"), "sub", None),
            P("groups", None, None),
            P("groups", None),
        ),
        out_specs=(P(("groups", "lat"), "sub", "tok"), P("sub", "tok", ("groups", "lat"))),
        check_vma=False,
    )
```

```python
import functools

import jax
import jax.numpy as jnp
from jax import lax
from jax.experimental import pallas as pl
from jax.experimental.pallas import tpu as pltpu
from jax.sharding import PartitionSpec as P

TBLK = 256
ORDER = {
    "w_far_in": ("codes",),
    "w_mid_in": ("codes",),
    "w_far": ("dec",),
    "sub_near": ("dec_far",),
    "tok_near_in": ("dec_far",),
    "w_2": ("enc_far_in",),
    "tok_rest": ("dec_pair_in", "dec_last_in",),
    "enc_mid": ("dec_pair",),
}
CONTRACT_LAST = (((1,), (1,)), ((), ()))
PLAIN = (((1,), (0,)), ((), ()))
CONTRACT_ROWS = (((0,), (0,)), ((), ()))


def dot32(left, right, dims):
    return lax.dot_general(left, right, dims, preferred_element_type=jnp.float32)


def local_call(body, out_shape, scalars, *args):
    vmem = pl.BlockSpec(memory_space=pltpu.VMEM)
    return pl.pallas_call(
        body,
        out_shape=out_shape,
        in_specs=[pl.BlockSpec(memory_space=pltpu.SMEM)] + [vmem] * len(args),
        out_specs=jax.tree.map(lambda _: vmem, out_shape),
        compiler_params=pltpu.CompilerParams(vmem_limit_bytes=12 * 2**20),
        cost_estimate=pl.CostEstimate(flops=0, bytes_accessed=0, transcendentals=0),
    )(jnp.stack(scalars).astype(jnp.int32), *args)


def turned(value):
    return value.astype(jnp.float32).T.astype(jnp.bfloat16)


def dec_body(block_ref, own_ref, other_ref, err_own_ref, err_other_ref, *out_refs):
    block = block_ref[0]
    total = dot32(turned(own_ref[block]), err_own_ref[...], PLAIN)
    total += dot32(turned(other_ref[block]), err_other_ref[...], PLAIN)
    for out_ref in out_refs:
        out_ref[...] = total.astype(out_ref.dtype)


def dlat_body(place_ref, own_ref, other_ref, *refs):
    place, out_ref = place_ref[0], refs[-1]
    for i, w_ref in enumerate(refs[:-1]):
        lanes = slice(i * w_ref.shape[0], (i + 1) * w_ref.shape[0])
        out_ref[place, :, lanes] = dot32(own_ref[...], w_ref[...], CONTRACT_LAST)
        out_ref[1 - place, :, lanes] = dot32(other_ref[...], w_ref[...], CONTRACT_LAST)


def enc_body(core_ref, acts_ref, mine_ref, other_ref, out_ref):
    core = core_ref[0]
    total = dot32(turned(mine_ref[...]), acts_ref[core], PLAIN)
    total += dot32(turned(other_ref[...]), acts_ref[1 - core], PLAIN)
    out_ref[...] = total.astype(out_ref.dtype)


def valid_ids(act_ids, act_count):
    slot = jnp.arange(act_ids.shape[2], dtype=jnp.int32)
    return jnp.where(slot[None, None, :] < act_count[:, :, None], act_ids, -1)


def row_hits(ids, first_row, rows, block):
    on = jnp.any(ids == block, axis=2)
    tile = (first_row + jnp.arange(rows, dtype=jnp.int32)) // TBLK
    hit = on[:, :, None] & (tile[None, None, :] == jnp.arange(ids.shape[1])[None, :, None])
    return jnp.any(hit, axis=1).astype(jnp.float32)


def shards_line(acts, err_grad, codes, dec_weight, act_ids, act_count):
    z = lax.axis_index("lat")
    x = lax.axis_index("tok")
    c = lax.axis_index("sub")
    rows = err_grad.shape[1]
    lat = dec_weight.shape[0]
    width = acts.shape[3]
    swap = [(0, 1), (1, 0)]
    pairs = [(0, 1), (1, 0), (2, 3), (3, 2)]
    inward, outward, across, ends = [(0, 1), (3, 2)], [(1, 0), (2, 3)], [(1, 2), (2, 1)], [(0, 3), (3, 0)]
    at_end = (z == 0) | (z == 3)

    ids = valid_ids(act_ids, act_count)
    act_rows = acts.reshape(2, rows, width)
    err_rows = err_grad.reshape(rows, -1)
    block = jax.ShapeDtypeStruct((lat, width), jnp.float32)
    block16 = jax.ShapeDtypeStruct((lat, width), jnp.bfloat16)
    steps, done = {}, {}

    def get(name):
        if name not in done:
            value = steps[name]()
            others = [get(other) for other in ORDER.get(name, ())]
            done[name] = lax.optimization_barrier((value, *others))[0] if others else value
        return done[name]

    def step(name, make):
        steps[name] = make

    def send(name, source, axis, pairs):
        step(name + "_in", source)
        step(name, lambda: lax.ppermute(get(name + "_in"), axis, pairs))

    def add32(term, got):
        return (term + got.astype(jnp.float32)).astype(jnp.bfloat16)

    step("weights", lambda: dec_weight.reshape(lat, -1))
    step("w_own", lambda: lax.dynamic_slice_in_dim(get("weights"), x * width, width, 1))
    send("w_1", lambda: get("w_own"), "lat", pairs)
    send("w_far", lambda: get("w_own"), "lat", ends)
    send("w_mid", lambda: get("w_own"), "lat", across)

    step("err_own", lambda: lax.dynamic_slice_in_dim(err_rows, x * width, width, 1))
    send("err", lambda: lax.dynamic_slice_in_dim(err_rows, (1 - x) * width, width, 1), "tok", swap)

    step("codes_in", lambda: codes.reshape(4, rows, lat))
    step("codes", lambda: lax.all_to_all(get("codes_in"), "lat", split_axis=0, concat_axis=0, tiled=True))
    send("codes_other", lambda: get("codes"), "tok", swap)

    def used(value, group):
        all_hits = jnp.stack([row_hits(ids, z * rows, rows, b) for b in range(4)])
        hit = lax.dynamic_index_in_dim(all_hits, group, 1, keepdims=False)
        return value * hit[:, :, None].astype(jnp.bfloat16)

    step("used_own", lambda: used(get("codes"), x))
    step("used_other", lambda: used(get("codes_other"), 1 - x))

    def dec_of(b, *out):
        codes_pair = get("used_own"), get("used_other")
        return local_call(dec_body, out, [b], *codes_pair, get("err_own"), get("err"))

    step("dec", lambda: dec_of(z ^ 3, block16))

    send("w_across", lambda: get("w_1"), "lat", across)
    send("w_out", lambda: get("w_mid"), "lat", outward)
    send("dec_far", lambda: get("dec")[0], "lat", inward)
    step("w_2", lambda: jnp.where(at_end, get("w_out"), get("w_across")))

    def latent_grads(tag, names, blocks):
        def part():
            weights = [get(name) for name in names]
            out = jax.ShapeDtypeStruct((2, rows, lat * len(weights)), jnp.float32)
            return local_call(dlat_body, out, [c ^ x], get("err_own"), get("err"), *weights)

        def mine():
            total, cols = get("sums" + tag) + get("tok" + tag), []
            for i, b in enumerate(blocks):
                hit = lax.dynamic_index_in_dim(row_hits(ids, z * rows, rows, b), c, 0, keepdims=False)
                cols.append((total[:, i * lat : (i + 1) * lat] * hit[:, None]).astype(jnp.bfloat16))
            return jnp.concatenate(cols, axis=1)

        step("part" + tag, part)
        send("sub" + tag, lambda: get("part" + tag)[1], "sub", swap)
        step("sums" + tag, lambda: get("part" + tag)[0] + get("sub" + tag))
        send("tok" + tag, lambda: get("sums" + tag), "tok", swap)
        step("mine" + tag, mine)
        send("other" + tag, lambda: get("mine" + tag), "sub", swap)

    latent_grads("_near", ["w_own", "w_far"], [z, z ^ 3])
    latent_grads("_rest", ["w_2", "w_mid", "w_1"], [z ^ 2, z ^ 3, z ^ 1])

    def enc_of(tag, pick, out=block):
        return local_call(enc_body, out, [c], act_rows, pick(get("mine" + tag)), pick(get("other" + tag)))

    def cols_of(i):
        return lambda part: part[:, i * lat : (i + 1) * lat]

    send("enc_far", lambda: enc_of("_near", cols_of(1), block16), "lat", inward)
    step("enc_own", lambda: enc_of("_near", cols_of(0)))
    step("enc_1", lambda: enc_of("_rest", cols_of(2)))
    step("enc_2", lambda: enc_of("_rest", cols_of(0)))
    step("enc_3", lambda: enc_of("_rest", cols_of(1)))
    for j, name in enumerate(("dec_own", "dec_1", "dec_2", "dec_3")):
        step(name, lambda j=j: dec_of(z ^ j, block)[0])

    def line_sums(kind):
        step(kind + "_two", lambda: add32(get(kind + "_2"), get(kind + "_far")))
        send(kind + "_in", lambda: get(kind + "_two"), "lat", inward)
        send(kind + "_mid", lambda: get(kind + "_two"), "lat", across)
        send(kind + "_pair", lambda: add32(get(kind + "_1"), get(kind + "_mid")), "lat", pairs)
        send(kind + "_last", lambda: add32(get(kind + "_3"), get(kind + "_in")), "lat", across)

    line_sums("dec")
    line_sums("enc")

    def total(kind):
        value = get(kind + "_own") + get(kind + "_pair").astype(jnp.float32) + get(kind + "_last").astype(jnp.float32)
        return value.astype(jnp.bfloat16)

    return total("dec")[:, None, :], total("enc").T[None]


def shards_any(acts, err_grad, codes, dec_weight, act_ids, act_count):
    z = lax.axis_index("lat")
    x = lax.axis_index("tok")
    rows = err_grad.shape[1]
    lat = dec_weight.shape[0]
    width = acts.shape[3]
    groups = acts.shape[0]
    blocks = lax.axis_size("lat")
    w_own = lax.dynamic_slice_in_dim(dec_weight.reshape(lat, -1), x * width, width, 1)
    w_all = lax.all_gather(w_own, "lat", axis=0, tiled=True)
    err = lax.all_to_all(err_grad, "tok", split_axis=3, concat_axis=0, tiled=True)
    err = err.reshape(groups * rows, width)
    ids = valid_ids(act_ids, act_count)
    code_hits = row_hits(lax.dynamic_slice_in_dim(ids, x, 1, 0), 0, codes.shape[1], z)
    used = codes[0] * code_hits.astype(jnp.bfloat16).T
    used = lax.all_to_all(used, "lat", split_axis=0, concat_axis=1, tiled=True)
    used = lax.all_gather(used, "tok", axis=0, tiled=True)
    dec_part = dot32(used, err, CONTRACT_ROWS)
    grad_dec = lax.psum_scatter(dec_part, "lat", scatter_dimension=0, tiled=True)
    dlat = lax.psum(dot32(err, w_all, CONTRACT_LAST), ("tok", "sub"))
    hits = [row_hits(ids, z * rows, rows, block).reshape(groups * rows, 1) for block in range(blocks)]
    hits = jnp.concatenate([jnp.broadcast_to(h, (groups * rows, lat)) for h in hits], axis=1)
    dcodes = (dlat * hits).astype(jnp.bfloat16)
    enc_part = dot32(acts.reshape(groups * rows, width), dcodes, CONTRACT_ROWS)
    grad_enc = lax.psum_scatter(enc_part, "lat", scatter_dimension=1, tiled=True)
    return grad_dec.astype(jnp.bfloat16)[:, None, :], grad_enc.astype(jnp.bfloat16)[None]


def solution(mesh):
    line = mesh.shape["lat"] == 4 and mesh.shape["tok"] == 2
    return jax.shard_map(
        shards_line if line else shards_any,
        mesh=mesh,
        in_specs=(
            P("groups", "lat", "sub", "tok"),
            P(("groups", "tok"), "lat", "sub", None),
            P(("groups", "tok"), None, "lat"),
            P(("groups", "lat"), "sub", None),
            P("groups", None, None),
            P("groups", None),
        ),
        out_specs=(P(("groups", "lat"), "sub", "tok"), P("sub", "tok", ("groups", "lat"))),
        check_vma=False,
    )
```

```python
import functools

import jax
import jax.numpy as jnp
from jax import lax
from jax.experimental import pallas as pl
from jax.experimental.pallas import tpu as pltpu
from jax.sharding import PartitionSpec as P

TBLK = 256
ORDER = {
    "w_far_in": ("codes",),
    "w_mid_in": ("codes",),
    "w_far": ("dec",),
    "sub_near": ("dec_far",),
    "tok_near_in": ("dec_far",),
    "w_across": ("tok_near", "w_out",),
    "w_2": ("enc_far_in",),
    "tok_rest": ("dec_pair_in", "dec_last_in",),
    "enc_mid": ("dec_pair",),
}
CONTRACT_LAST = (((1,), (1,)), ((), ()))
PLAIN = (((1,), (0,)), ((), ()))
CONTRACT_ROWS = (((0,), (0,)), ((), ()))


def dot32(left, right, dims):
    return lax.dot_general(left, right, dims, preferred_element_type=jnp.float32)


def local_call(body, out_shape, scalars, *args):
    vmem = pl.BlockSpec(memory_space=pltpu.VMEM)
    return pl.pallas_call(
        body,
        out_shape=out_shape,
        in_specs=[pl.BlockSpec(memory_space=pltpu.SMEM)] + [vmem] * len(args),
        out_specs=jax.tree.map(lambda _: vmem, out_shape),
        compiler_params=pltpu.CompilerParams(vmem_limit_bytes=12 * 2**20),
        cost_estimate=pl.CostEstimate(flops=0, bytes_accessed=0, transcendentals=0),
    )(jnp.stack(scalars).astype(jnp.int32), *args)


def turned(value):
    return value.astype(jnp.float32).T.astype(jnp.bfloat16)


def dec_body(block_ref, own_ref, other_ref, err_own_ref, err_other_ref, *out_refs):
    block = block_ref[0]
    total = dot32(turned(own_ref[block]), err_own_ref[...], PLAIN)
    total += dot32(turned(other_ref[block]), err_other_ref[...], PLAIN)
    for out_ref in out_refs:
        out_ref[...] = total.astype(out_ref.dtype)


def dlat_body(place_ref, own_ref, other_ref, *refs):
    place, out_ref = place_ref[0], refs[-1]
    for i, w_ref in enumerate(refs[:-1]):
        lanes = slice(i * w_ref.shape[0], (i + 1) * w_ref.shape[0])
        out_ref[place, :, lanes] = dot32(own_ref[...], w_ref[...], CONTRACT_LAST)
        out_ref[1 - place, :, lanes] = dot32(other_ref[...], w_ref[...], CONTRACT_LAST)


def enc_body(core_ref, acts_ref, mine_ref, other_ref, out_ref):
    core = core_ref[0]
    total = dot32(turned(mine_ref[...]), acts_ref[core], PLAIN)
    total += dot32(turned(other_ref[...]), acts_ref[1 - core], PLAIN)
    out_ref[...] = total.astype(out_ref.dtype)


def valid_ids(act_ids, act_count):
    slot = jnp.arange(act_ids.shape[2], dtype=jnp.int32)
    return jnp.where(slot[None, None, :] < act_count[:, :, None], act_ids, -1)


def row_hits(ids, first_row, rows, block):
    on = jnp.any(ids == block, axis=2)
    tile = (first_row + jnp.arange(rows, dtype=jnp.int32)) // TBLK
    hit = on[:, :, None] & (tile[None, None, :] == jnp.arange(ids.shape[1])[None, :, None])
    return jnp.any(hit, axis=1).astype(jnp.float32)


def shards_line(acts, err_grad, codes, dec_weight, act_ids, act_count):
    z = lax.axis_index("lat")
    x = lax.axis_index("tok")
    c = lax.axis_index("sub")
    rows = err_grad.shape[1]
    lat = dec_weight.shape[0]
    width = acts.shape[3]
    swap = [(0, 1), (1, 0)]
    pairs = [(0, 1), (1, 0), (2, 3), (3, 2)]
    inward, outward, across, ends = [(0, 1), (3, 2)], [(1, 0), (2, 3)], [(1, 2), (2, 1)], [(0, 3), (3, 0)]
    at_end = (z == 0) | (z == 3)

    ids = valid_ids(act_ids, act_count)
    act_rows = acts.reshape(2, rows, width)
    err_rows = err_grad.reshape(rows, -1)
    block = jax.ShapeDtypeStruct((lat, width), jnp.float32)
    block16 = jax.ShapeDtypeStruct((lat, width), jnp.bfloat16)
    steps, done = {}, {}

    def get(name):
        if name not in done:
            value = steps[name]()
            others = [get(other) for other in ORDER.get(name, ())]
            done[name] = lax.optimization_barrier((value, *others))[0] if others else value
        return done[name]

    def step(name, make):
        steps[name] = make

    def send(name, source, axis, pairs):
        step(name + "_in", source)
        step(name, lambda: lax.ppermute(get(name + "_in"), axis, pairs))

    def add32(term, got):
        return (term + got.astype(jnp.float32)).astype(jnp.bfloat16)

    step("weights", lambda: dec_weight.reshape(lat, -1))
    step("w_own", lambda: lax.dynamic_slice_in_dim(get("weights"), x * width, width, 1))
    send("w_1", lambda: get("w_own"), "lat", pairs)
    send("w_far", lambda: get("w_own"), "lat", ends)
    send("w_mid", lambda: get("w_own"), "lat", across)

    step("err_own", lambda: lax.dynamic_slice_in_dim(err_rows, x * width, width, 1))
    send("err", lambda: lax.dynamic_slice_in_dim(err_rows, (1 - x) * width, width, 1), "tok", swap)

    step("codes_in", lambda: codes.reshape(4, rows, lat))
    step("codes", lambda: lax.all_to_all(get("codes_in"), "lat", split_axis=0, concat_axis=0, tiled=True))
    send("codes_other", lambda: get("codes"), "tok", swap)

    def used(value, group):
        all_hits = jnp.stack([row_hits(ids, z * rows, rows, b) for b in range(4)])
        hit = lax.dynamic_index_in_dim(all_hits, group, 1, keepdims=False)
        return value * hit[:, :, None].astype(jnp.bfloat16)

    step("used_own", lambda: used(get("codes"), x))
    step("used_other", lambda: used(get("codes_other"), 1 - x))

    def dec_of(b, *out):
        codes_pair = get("used_own"), get("used_other")
        return local_call(dec_body, out, [b], *codes_pair, get("err_own"), get("err"))

    step("dec", lambda: dec_of(z ^ 3, block16))

    send("w_across", lambda: get("w_1"), "lat", across)
    send("w_out", lambda: get("w_mid"), "lat", outward)
    send("dec_far", lambda: get("dec")[0], "lat", inward)
    step("w_2", lambda: jnp.where(at_end, get("w_out"), get("w_across")))

    def latent_grads(tag, names, blocks):
        def part():
            weights = [get(name) for name in names]
            out = jax.ShapeDtypeStruct((2, rows, lat * len(weights)), jnp.float32)
            return local_call(dlat_body, out, [c ^ x], get("err_own"), get("err"), *weights)

        def mine():
            total, cols = get("sums" + tag) + get("tok" + tag), []
            for i, b in enumerate(blocks):
                hit = lax.dynamic_index_in_dim(row_hits(ids, z * rows, rows, b), c, 0, keepdims=False)
                cols.append((total[:, i * lat : (i + 1) * lat] * hit[:, None]).astype(jnp.bfloat16))
            return jnp.concatenate(cols, axis=1)

        step("part" + tag, part)
        send("sub" + tag, lambda: get("part" + tag)[1], "sub", swap)
        step("sums" + tag, lambda: get("part" + tag)[0] + get("sub" + tag))
        send("tok" + tag, lambda: get("sums" + tag), "tok", swap)
        step("mine" + tag, mine)
        send("other" + tag, lambda: get("mine" + tag), "sub", swap)

    latent_grads("_near", ["w_own", "w_far"], [z, z ^ 3])
    latent_grads("_rest", ["w_2", "w_mid", "w_1"], [z ^ 2, z ^ 3, z ^ 1])

    def enc_of(tag, pick, out=block):
        return local_call(enc_body, out, [c], act_rows, pick(get("mine" + tag)), pick(get("other" + tag)))

    def cols_of(i):
        return lambda part: part[:, i * lat : (i + 1) * lat]

    send("enc_far", lambda: enc_of("_near", cols_of(1), block16), "lat", inward)
    step("enc_own", lambda: enc_of("_near", cols_of(0)))
    step("enc_1", lambda: enc_of("_rest", cols_of(2)))
    step("enc_2", lambda: enc_of("_rest", cols_of(0)))
    step("enc_3", lambda: enc_of("_rest", cols_of(1)))
    for j, name in enumerate(("dec_own", "dec_1", "dec_2", "dec_3")):
        step(name, lambda j=j: dec_of(z ^ j, block)[0])

    def line_sums(kind):
        step(kind + "_two", lambda: add32(get(kind + "_2"), get(kind + "_far")))
        send(kind + "_in", lambda: get(kind + "_two"), "lat", inward)
        send(kind + "_mid", lambda: get(kind + "_two"), "lat", across)
        send(kind + "_pair", lambda: add32(get(kind + "_1"), get(kind + "_mid")), "lat", pairs)
        send(kind + "_last", lambda: add32(get(kind + "_3"), get(kind + "_in")), "lat", across)

    line_sums("dec")
    line_sums("enc")

    def total(kind):
        value = get(kind + "_own") + get(kind + "_pair").astype(jnp.float32) + get(kind + "_last").astype(jnp.float32)
        return value.astype(jnp.bfloat16)

    return total("dec")[:, None, :], total("enc").T[None]


def shards_any(acts, err_grad, codes, dec_weight, act_ids, act_count):
    z = lax.axis_index("lat")
    x = lax.axis_index("tok")
    rows = err_grad.shape[1]
    lat = dec_weight.shape[0]
    width = acts.shape[3]
    groups = acts.shape[0]
    blocks = lax.axis_size("lat")
    w_own = lax.dynamic_slice_in_dim(dec_weight.reshape(lat, -1), x * width, width, 1)
    w_all = lax.all_gather(w_own, "lat", axis=0, tiled=True)
    err = lax.all_to_all(err_grad, "tok", split_axis=3, concat_axis=0, tiled=True)
    err = err.reshape(groups * rows, width)
    ids = valid_ids(act_ids, act_count)
    code_hits = row_hits(lax.dynamic_slice_in_dim(ids, x, 1, 0), 0, codes.shape[1], z)
    used = codes[0] * code_hits.astype(jnp.bfloat16).T
    used = lax.all_to_all(used, "lat", split_axis=0, concat_axis=1, tiled=True)
    used = lax.all_gather(used, "tok", axis=0, tiled=True)
    dec_part = dot32(used, err, CONTRACT_ROWS)
    grad_dec = lax.psum_scatter(dec_part, "lat", scatter_dimension=0, tiled=True)
    dlat = lax.psum(dot32(err, w_all, CONTRACT_LAST), ("tok", "sub"))
    hits = [row_hits(ids, z * rows, rows, block).reshape(groups * rows, 1) for block in range(blocks)]
    hits = jnp.concatenate([jnp.broadcast_to(h, (groups * rows, lat)) for h in hits], axis=1)
    dcodes = (dlat * hits).astype(jnp.bfloat16)
    enc_part = dot32(acts.reshape(groups * rows, width), dcodes, CONTRACT_ROWS)
    grad_enc = lax.psum_scatter(enc_part, "lat", scatter_dimension=1, tiled=True)
    return grad_dec.astype(jnp.bfloat16)[:, None, :], grad_enc.astype(jnp.bfloat16)[None]


def solution(mesh):
    line = mesh.shape["lat"] == 4 and mesh.shape["tok"] == 2
    return jax.shard_map(
        shards_line if line else shards_any,
        mesh=mesh,
        in_specs=(
            P("groups", "lat", "sub", "tok"),
            P(("groups", "tok"), "lat", "sub", None),
            P(("groups", "tok"), None, "lat"),
            P(("groups", "lat"), "sub", None),
            P("groups", None, None),
            P("groups", None),
        ),
        out_specs=(P(("groups", "lat"), "sub", "tok"), P("sub", "tok", ("groups", "lat"))),
        check_vma=False,
    )
```
